32 devices in a mesh: groups: 2 (over y), tiles: 4 (over z), section: 4 (over x, core).
Axes of the slice: x: 2, y: 2, z: 4, core: 2. Of those that a mesh axis runs over, the one named last changes fastest.
Arguments:
- latents: float32 [4, 192, 8, 128], P('groups', None, 'tiles'), parts along dimension 0, may hold values from -6 to 6
- conv_weight: float32 [4, 27, 192, 192], P('section'), may hold values from -0.078125 to 0.078125
- gain: float32 [4, 192], P('section'), may hold values from 0.1 to 1.9
Outputs:
- decoded: float32 [4, 192, 8, 128], P('groups', 'section', 'tiles'), parts along dimension 0
The draws below stay inside these ranges and needn't reach their ends.
There are 2 independent parts, one for each index of `groups`. The reference program is written for one: setup_inputs(seed, part) draws one part's arguments, and reference() takes and returns one part's arrays. A program takes and returns all parts, laid end to end along the dimension named above; an argument that names none is the same for every part. Nothing has to cross between parts.
All inputs are finite; a program needn't handle non-finite values.
Results may differ from the reference program's by a relative error of at most 0.00013.
Values sent between devices are 32-bit elements; how exact they have to be, the bound alone decides.
A program may use at most 64 MiB of HBM per device.

```python
import jax
import jax.numpy as jnp
from jax import lax

C = 192
W = 128
FRAMES = 2
LAYERS = 4
HEIGHT = 8


def block_scale(stream_key, extent, cuts, low, high):
    level = 1.0
    for position, parts in cuts:
        steps = jax.random.uniform(jax.random.fold_in(jax.random.fold_in(stream_key, 6), position), (parts,), jnp.float32, low / len(cuts), high / len(cuts))
        level = level * jnp.repeat(jnp.exp(steps), extent[position] // parts).reshape((-1,) + (1,) * (len(extent) - 1 - position))
    return level


def scatter_about(own_key, dims, deviation, limit, shards=(), kind=jnp.bfloat16):
    values = jax.random.normal(own_key, dims, jnp.float32) * deviation
    if len(shards) > 0:
        values = block_scale(own_key, dims, shards, -0.22, 0.18) * values
    return jnp.clip(values, min=-limit, max=limit).astype(kind)


def setup_inputs(seed: int = 0, part: int = 0) -> dict:
    key_of = jax.random.split(jax.random.key(seed), 4)
    part_splits = jax.random.split(jax.random.fold_in(key_of[3], part), 4)
    latents = scatter_about(part_splits[0], (FRAMES, C, HEIGHT, W), 1.0, 6.0, ((2, 4),), jnp.float32)
    conv_weight = scatter_about(key_of[1], (LAYERS, 27, C, C), (27 * C) ** -0.5, 0.078125, ((0, 4),), jnp.float32)
    gain = jnp.clip(1.0 + 0.18 * jax.random.normal(key_of[2], (LAYERS, C), jnp.float32), 0.1, 1.9)
    return dict(latents=latents, conv_weight=conv_weight, gain=gain)


def normalize(values, gain_row):
    meansq = lax.optimization_barrier(jnp.mean(values * values, axis=1, keepdims=True))
    scaled = values * lax.rsqrt(meansq + 1e-06) * gain_row[None, :, None, None]
    return jax.nn.silu(scaled)

def reference(latents, conv_weight, gain):
    current = latents
    for layer in range(LAYERS):
        normed = normalize(current, gain[layer])
        kernel = conv_weight[layer].reshape(3, 3, 3, C, C).transpose(3, 4, 0, 1, 2)
        inputs = normed.transpose(1, 0, 2, 3)[None]
        result = lax.conv_general_dilated(inputs, kernel, (1, 1, 1), ((2, 0), (1, 1), (1, 1)), dimension_numbers=('NCDHW', 'OIDHW', 'NCDHW'), precision=lax.Precision.HIGHEST)
        current = current + result[0].transpose(1, 0, 2, 3)
    return current
```

```python
import functools

import jax
import jax.numpy as jnp
from jax import lax
from jax.experimental import pallas as pl
from jax.experimental.pallas import tpu as pltpu
from jax.sharding import PartitionSpec as P

EPSILON = 1e-06
MESH = pl.DeviceIdType.MESH


def halves(value):
    high = value.astype(jnp.bfloat16)
    low = (value - high.astype(jnp.float32)).astype(jnp.bfloat16)
    return high, low


def kernel(
    dims,
    lat_ref, weight_ref, gain_ref, out_ref,
    raw, w_high, w_low, main, halo, n_high, n_low, acc, result, stage, gain_col,
    weight_sem, main_send, main_recv, halo_send, halo_recv, out_send, out_recv, own_sem,
):
    frames, rows, channels, cols, layers, tiles, first_tap = dims
    share = channels // layers
    section = lax.axis_index("section")
    tile = lax.axis_index("tiles")
    last = layers - 1
    has_up = tile > 0
    has_down = tile < tiles - 1
    taps = 3 - first_tap

    def weight_copy(a, b):
        return pltpu.make_async_copy(
            weight_ref.at[0, pl.ds(9 * (a + first_tap) + 3 * b, 3)],
            raw.at[a, b],
            weight_sem.at[a, b],
        )

    order = [(a, b) for a in reversed(range(taps)) for b in (1, 0, 2)]
    for a, b in order:
        weight_copy(a, b).start()

    barrier = pltpu.get_barrier_semaphore()

    def greet(condition, target):
        @pl.when(condition)
        def _():
            pl.semaphore_signal(barrier, inc=1, device_id=target, device_id_type=MESH)

    links = [
        (has_up, {"tiles": tile - 1}),
        (has_down, {"tiles": tile + 1}),
        (section > 0, {"section": section - 1}),
        (section < last, {"section": section + 1}),
        (section < last, {"section": last}),
    ]
    links += [(section == last, {"section": peer}) for peer in range(last)]
    for condition, target in links:
        greet(condition, target)

    def up_copy(f):
        return pltpu.make_async_remote_copy(
            src_ref=main.at[f, 0], dst_ref=halo.at[f, 1],
            send_sem=halo_send.at[f, 0], recv_sem=halo_recv.at[f, 1],
            device_id={"tiles": tile - 1}, device_id_type=MESH,
        )

    def down_copy(f):
        return pltpu.make_async_remote_copy(
            src_ref=main.at[f, rows - 1], dst_ref=halo.at[f, 0],
            send_sem=halo_send.at[f, 1], recv_sem=halo_recv.at[f, 0],
            device_id={"tiles": tile + 1}, device_id_type=MESH,
        )

    def main_copy(f):
        return pltpu.make_async_remote_copy(
            src_ref=result.at[f], dst_ref=main.at[f],
            send_sem=main_send.at[f], recv_sem=main_recv.at[f],
            device_id={"section": section + 1}, device_id_type=MESH,
        )

    def out_copy(f, peer):
        return pltpu.make_async_remote_copy(
            src_ref=stage.at[f, pl.ds(peer * share * rows, share * rows)],
            dst_ref=out_ref.at[f],
            send_sem=out_send.at[f, peer], recv_sem=out_recv.at[f],
            device_id={"section": peer}, device_id_type=MESH,
        )

    def own_copy(f):
        return pltpu.make_async_copy(
            stage.at[f, pl.ds(last * share * rows, share * rows)], out_ref.at[f], own_sem.at[f]
        )

    def send_edges(f):
        @pl.when(has_up)
        def _():
            up_copy(f).start()

        @pl.when(has_down)
        def _():
            down_copy(f).start()

    @pl.when(section == 0)
    def _():
        for f in range(frames):
            for r in range(rows):
                main[f, r] = lat_ref[f, pl.ds(r, channels, stride=rows), :]

    @pl.when(jnp.logical_not(has_up))
    def _():
        for f in range(frames):
            halo[f, 0] = jnp.zeros((channels, cols), jnp.float32)

    @pl.when(jnp.logical_not(has_down))
    def _():
        for f in range(frames):
            halo[f, 1] = jnp.zeros((channels, cols), jnp.float32)

    pl.semaphore_wait(barrier, sum(condition.astype(jnp.int32) for condition, _ in links))

    @pl.when(section == 0)
    def _():
        for f in range(frames):
            send_edges(f)

    diagonal = lax.broadcasted_iota(jnp.int32, (channels, channels), 0) == (
        lax.broadcasted_iota(jnp.int32, (channels, channels), 1)
    )
    column = jnp.sum(
        jnp.where(diagonal, jnp.broadcast_to(gain_ref[0:1, :], (channels, channels)), 0.0),
        axis=1, keepdims=True,
    )
    gain_col[...] = jnp.broadcast_to(column, (channels, cols))

    for a, b in order:
        weight_copy(a, b).wait()
        for e in range(3):
            high, low = halves(raw[a, b, e])
            w_high[a, b, pl.ds(e * channels, channels), :] = high
            w_low[a, b, pl.ds(e * channels, channels), :] = low

    def normalize(values, f, place):
        meansq = jnp.mean(values * values, axis=0, keepdims=True)
        scaled = values * lax.rsqrt(meansq + EPSILON) * gain_col[...]
        high, low = halves(scaled / (1.0 + jnp.exp(-scaled)))
        n_high[f, place] = high
        n_low[f, place] = low

    def add_taps(f, a, offsets, fresh):
        source = f - 2 + a + first_tap
        total = None
        for b in offsets:
            high = jnp.concatenate([n_high[source, r + b] for r in range(rows)], axis=1)
            low = jnp.concatenate([n_low[source, r + b] for r in range(rows)], axis=1)
            part = jnp.dot(w_high[a, b], high, preferred_element_type=jnp.float32)
            part += jnp.dot(w_low[a, b], high, preferred_element_type=jnp.float32)
            part += jnp.dot(w_high[a, b], low, preferred_element_type=jnp.float32)
            total = part if total is None else total + part
        if fresh:
            acc[f] = total
        else:
            acc[f] = acc[f] + total

    lane = lax.broadcasted_iota(jnp.int32, (channels, cols), 1)

    for f in range(frames):
        fresh = True
        for a in range(taps - 1):
            if f - 2 + a + first_tap >= 0:
                add_taps(f, a, (0, 1, 2), fresh)
                fresh = False

        @pl.when(section > 0)
        def _():
            main_copy(f).wait_recv()
            send_edges(f)

        for r in range(rows):
            normalize(main[f, r], f, r + 1)
        add_taps(f, taps - 1, (1,), fresh)

        @pl.when(has_up)
        def _():
            down_copy(f).wait_recv()

        @pl.when(has_down)
        def _():
            up_copy(f).wait_recv()

        normalize(halo[f, 0], f, 0)
        normalize(halo[f, 1], f, rows + 1)
        add_taps(f, taps - 1, (0, 2), False)
        for r in range(rows):
            here = pl.ds(r * cols, cols)
            before = pltpu.roll(acc[f, pl.ds(0, channels), here], 1, 1)
            after = pltpu.roll(acc[f, pl.ds(2 * channels, channels), here], cols - 1, 1)
            result[f, r] = (
                main[f, r]
                + acc[f, pl.ds(channels, channels), here]
                + jnp.where(lane > 0, before, 0.0)
                + jnp.where(lane < cols - 1, after, 0.0)
            )

        @pl.when(section < last)
        def _():
            main_copy(f).start()

        @pl.when(section == last)
        def _():
            for r in range(rows):
                stage[f, pl.ds(r, channels, stride=rows), :] = result[f, r]
            for peer in range(last):
                out_copy(f, peer).start()
            own_copy(f).start()

    for f in range(frames):
        @pl.when(has_up)
        def _():
            up_copy(f).wait_send()

        @pl.when(has_down)
        def _():
            down_copy(f).wait_send()

        @pl.when(section < last)
        def _():
            main_copy(f).wait_send()

        @pl.when(section == last)
        def _():
            for peer in range(last):
                out_copy(f, peer).wait_send()
            own_copy(f).wait()

    @pl.when(section < last)
    def _():
        for f in range(frames):
            out_copy(f, 0).wait_recv()


def local(latents, conv_weight, gain):
    frames, channels, rows, cols = latents.shape
    layers = lax.axis_size("section")
    tiles = lax.axis_size("tiles")
    share = channels // layers
    first_tap = max(0, 3 - frames)
    taps = 3 - first_tap
    f32, bf16 = jnp.float32, jnp.bfloat16
    dma = pltpu.SemaphoreType.DMA
    macs = frames * rows * cols * channels * channels * 27
    out = pl.pallas_call(
        functools.partial(kernel, (frames, rows, channels, cols, layers, tiles, first_tap)),
        out_shape=jax.ShapeDtypeStruct((frames, share * rows, cols), f32),
        in_specs=[
            pl.BlockSpec(memory_space=pltpu.VMEM),
            pl.BlockSpec(memory_space=pltpu.HBM),
            pl.BlockSpec(memory_space=pltpu.VMEM),
        ],
        out_specs=pl.BlockSpec(memory_space=pltpu.HBM),
        scratch_shapes=[
            pltpu.VMEM((taps, 3, 3, channels, channels), f32),
            pltpu.VMEM((taps, 3, 3 * channels, channels), bf16),
            pltpu.VMEM((taps, 3, 3 * channels, channels), bf16),
            pltpu.VMEM((frames, rows, channels, cols), f32),
            pltpu.VMEM((frames, 2, channels, cols), f32),
            pltpu.VMEM((frames, rows + 2, channels, cols), bf16),
            pltpu.VMEM((frames, rows + 2, channels, cols), bf16),
            pltpu.VMEM((frames, 3 * channels, rows * cols), f32),
            pltpu.VMEM((frames, rows, channels, cols), f32),
            pltpu.VMEM((frames, channels * rows, cols), f32),
            pltpu.VMEM((channels, cols), f32),
            dma((taps, 3)),
            dma((frames,)),
            dma((frames,)),
            dma((frames, 2)),
            dma((frames, 2)),
            dma((frames, layers)),
            dma((frames,)),
            dma((frames,)),
        ],
        compiler_params=pltpu.CompilerParams(
            collective_id=0, has_side_effects=True, vmem_limit_bytes=48 * 1024 * 1024
        ),
        cost_estimate=pl.CostEstimate(
            flops=6 * macs, bytes_accessed=4 * conv_weight.size, transcendentals=latents.size
        ),
    )(latents.reshape(frames, channels * rows, cols), conv_weight, gain)
    return out.reshape(frames, share, rows, cols)


def solution(mesh):
    return jax.shard_map(
        local,
        mesh=mesh,
        in_specs=(
            P("groups", None, "tiles", None),
            P("section", None, None, None),
            P("section", None),
        ),
        out_specs=P("groups", "section", "tiles", None),
        check_vma=False,
    )
```

```python
import functools

import jax
import jax.numpy as jnp
from jax import lax
from jax.experimental import pallas as pl
from jax.experimental.pallas import tpu as pltpu
from jax.sharding import PartitionSpec as P

EPSILON = 1e-06
MESH = pl.DeviceIdType.MESH


def halves(value):
    high = value.astype(jnp.bfloat16)
    low = (value - high.astype(jnp.float32)).astype(jnp.bfloat16)
    return high, low


def kernel(
    dims,
    lat_ref, weight_ref, gain_ref, out_ref,
    lat, raw, gain_row, weights, main, halo, normed, acc, result, stage, gain_col,
    lat_sem, gain_sem, weight_sem, main_send, main_recv, edge_send, edge_recv,
    out_send, out_recv, own_sem,
):
    frames, rows, channels, cols, layers, tiles, first_tap, chunks, depth = dims
    share = channels // layers
    part = channels // chunks
    section = lax.axis_index("section")
    tile = lax.axis_index("tiles")
    last = layers - 1
    has_up = tile > 0
    has_down = tile < tiles - 1
    taps = 3 - first_tap
    even = section % 2 == 0
    direct_out = even & (section < last)
    sides = ((has_up, -1), (has_down, 1))

    def weight_copy(a, b):
        return pltpu.make_async_copy(
            weight_ref.at[0, pl.ds(9 * (a + first_tap) + 3 * b, 3)],
            raw.at[a, b],
            weight_sem.at[a, b],
        )

    lat_copy = pltpu.make_async_copy(lat_ref, lat, lat_sem)
    gain_copy = pltpu.make_async_copy(gain_ref, gain_row, gain_sem)

    @pl.when(section == 0)
    def _():
        lat_copy.start()

    gain_copy.start()
    order = [(a, b) for a in reversed(range(taps)) for b in (1, 0, 2)]
    for a, b in order:
        weight_copy(a, b).start()

    barrier = pltpu.get_barrier_semaphore()
    links = [
        (section > 0, {"section": section - 1}),
        (section < last, {"section": section + 1}),
        (section < last, {"section": last}),
    ]
    links += [(section == last, {"section": peer}) for peer in range(last)]
    for present, step in sides:
        links.append((present & even, {"tiles": tile + step}))
        links.append((present & direct_out, {"tiles": tile + step, "section": section + 1}))
        links.append(
            (present & jnp.logical_not(even), {"tiles": tile + step, "section": section - 1})
        )

    def greet(condition, target):
        @pl.when(condition)
        def _():
            pl.semaphore_signal(barrier, inc=1, device_id=target, device_id_type=MESH)

    for condition, target in links:
        greet(condition, target)

    def piece(k):
        return pl.ds(k * part, part)

    def edge_copy(f, k, side, direct):
        source = result if direct else main
        target = {"tiles": tile + sides[side][1]}
        if direct:
            target["section"] = section + 1
        return pltpu.make_async_remote_copy(
            src_ref=source.at[f, 0 if side == 0 else rows - 1, piece(k)],
            dst_ref=halo.at[f, 1 - side, piece(k)],
            send_sem=edge_send.at[f, k, side, int(direct)],
            recv_sem=edge_recv.at[f, k, 1 - side],
            device_id=target, device_id_type=MESH,
        )

    def main_copy(f, k):
        return pltpu.make_async_remote_copy(
            src_ref=result.at[f, :, piece(k)], dst_ref=main.at[f, :, piece(k)],
            send_sem=main_send.at[f, k], recv_sem=main_recv.at[f, k],
            device_id={"section": section + 1}, device_id_type=MESH,
        )

    def out_copy(f, peer):
        return pltpu.make_async_remote_copy(
            src_ref=stage.at[f, pl.ds(peer * share * rows, share * rows)],
            dst_ref=out_ref.at[f],
            send_sem=out_send.at[f, peer], recv_sem=out_recv.at[f],
            device_id={"section": peer}, device_id_type=MESH,
        )

    def own_copy(f):
        return pltpu.make_async_copy(
            stage.at[f, pl.ds(last * share * rows, share * rows)], out_ref.at[f], own_sem.at[f]
        )

    def send_edges(f, k, direct):
        for side, (present, _) in enumerate(sides):
            @pl.when(present)
            def _():
                edge_copy(f, k, side, direct).start()

    @pl.when(section == 0)
    def _():
        lat_copy.wait()
        for f in range(frames):
            for r in range(rows):
                main[f, r] = lat[f, pl.ds(r, channels, stride=rows), :]

    for side, (present, _) in enumerate(sides):
        @pl.when(jnp.logical_not(present))
        def _():
            for f in range(frames):
                halo[f, side] = jnp.zeros((channels, cols), jnp.float32)

    pl.semaphore_wait(barrier, sum(condition.astype(jnp.int32) for condition, _ in links))

    @pl.when(section == 0)
    def _():
        for f in range(frames):
            for k in range(chunks):
                send_edges(f, k, False)

    gain_copy.wait()
    diagonal = lax.broadcasted_iota(jnp.int32, (channels, channels), 0) == (
        lax.broadcasted_iota(jnp.int32, (channels, channels), 1)
    )
    column = jnp.sum(
        jnp.where(diagonal, jnp.broadcast_to(gain_row[0:1, :], (channels, channels)), 0.0),
        axis=1, keepdims=True,
    )
    gain_col[...] = jnp.broadcast_to(column, (channels, cols))

    blank = jnp.zeros((depth - channels, cols), jnp.bfloat16)
    for f in range(frames):
        for r in range(rows + 2):
            for h in range(2):
                normed[f, r, h, pl.ds(channels, depth - channels), :] = blank

    rim = jnp.zeros((channels, depth - channels), jnp.bfloat16)
    for a, b in order:
        weight_copy(a, b).wait()
        for e in range(3):
            for h, half in enumerate(halves(raw[a, b, e])):
                half = jnp.concatenate([half, rim], axis=1)
                for k in range(chunks):
                    weights[
                        h, a, pl.ds((3 * k + e) * part, part), pl.ds(b * depth, depth)
                    ] = half[k * part : (k + 1) * part]

    def normalize(values, f, place):
        meansq = jnp.mean(values * values, axis=0, keepdims=True)
        scaled = values * lax.rsqrt(meansq + EPSILON) * gain_col[...]
        for h, half in enumerate(halves(scaled / (1.0 + jnp.exp(-scaled)))):
            normed[f, place, h, pl.ds(0, channels), :] = half

    def product(f, a, offsets, first, count):
        source = f - 2 + a + first_tap
        left = [
            weights[h, a, pl.ds(first, count), pl.ds(b * depth, depth)]
            for h in (0, 1, 0) for b in offsets
        ]
        right = [
            jnp.concatenate([normed[source, r + b, h] for r in range(rows)], axis=1)
            for h in (0, 0, 1) for b in offsets
        ]
        return jnp.dot(
            jnp.concatenate(left, axis=1),
            jnp.concatenate(right, axis=0),
            preferred_element_type=jnp.float32,
        )

    lane = lax.broadcasted_iota(jnp.int32, (part, cols), 1)

    for f in range(frames):
        fresh = True
        for a in range(taps - 1):
            if f - 2 + a + first_tap >= 0:
                value = product(f, a, (0, 1, 2), 0, 3 * channels)
                acc[f] = value if fresh else acc[f] + value
                fresh = False

        @pl.when(section > 0)
        def _():
            for k in range(chunks):
                main_copy(f, k).wait_recv()

                @pl.when(even)
                def _():
                    send_edges(f, k, False)

        for r in range(rows):
            normalize(main[f, r], f, r + 1)
        value = product(f, taps - 1, (1,), 0, 3 * channels)
        acc[f] = value if fresh else acc[f] + value

        for side, (present, _) in enumerate(sides):
            @pl.when(present)
            def _():
                for k in range(chunks):
                    edge_copy(f, k, 1 - side, False).wait_recv()

        normalize(halo[f, 0], f, 0)
        normalize(halo[f, 1], f, rows + 1)
        for k in range(chunks):
            base = 3 * k * part
            value = acc[f, pl.ds(base, 3 * part), :] + product(
                f, taps - 1, (0, 2), base, 3 * part
            )
            for r in range(rows):
                span = slice(r * cols, (r + 1) * cols)
                before = pltpu.roll(value[:part, span], 1, 1)
                after = pltpu.roll(value[2 * part :, span], cols - 1, 1)
                result[f, r, piece(k)] = (
                    main[f, r, piece(k)]
                    + value[part : 2 * part, span]
                    + jnp.where(lane > 0, before, 0.0)
                    + jnp.where(lane < cols - 1, after, 0.0)
                )

            @pl.when(section < last)
            def _():
                @pl.when(even)
                def _():
                    send_edges(f, k, True)

                main_copy(f, k).start()

            @pl.when(section == last)
            def _():
                for r in range(rows):
                    stage[f, pl.ds(k * part * rows + r, part, stride=rows), :] = result[
                        f, r, piece(k)
                    ]
                for peer in range(k * layers // chunks, (k + 1) * layers // chunks):
                    if peer < last:
                        out_copy(f, peer).start()
                    else:
                        own_copy(f).start()

    for f in range(frames):
        for k in range(chunks):
            for side, (present, _) in enumerate(sides):
                @pl.when(present & even)
                def _():
                    edge_copy(f, k, side, False).wait_send()

                @pl.when(present & direct_out)
                def _():
                    edge_copy(f, k, side, True).wait_send()

            @pl.when(section < last)
            def _():
                main_copy(f, k).wait_send()

        @pl.when(section == last)
        def _():
            for peer in range(last):
                out_copy(f, peer).wait_send()
            own_copy(f).wait()

    @pl.when(section < last)
    def _():
        for f in range(frames):
            out_copy(f, 0).wait_recv()


def local(latents, conv_weight, gain):
    frames, channels, rows, cols = latents.shape
    layers = lax.axis_size("section")
    tiles = lax.axis_size("tiles")
    share = channels // layers
    first_tap = max(0, 3 - frames)
    taps = 3 - first_tap
    chunks = 2
    depth = -(-channels // 256) * 256
    f32, bf16 = jnp.float32, jnp.bfloat16
    dma = pltpu.SemaphoreType.DMA
    macs = frames * rows * cols * channels * channels * 27
    dims = (frames, rows, channels, cols, layers, tiles, first_tap, chunks, depth)
    out = pl.pallas_call(
        functools.partial(kernel, dims),
        out_shape=jax.ShapeDtypeStruct((frames, share * rows, cols), f32),
        in_specs=[pl.BlockSpec(memory_space=pltpu.HBM)] * 3,
        out_specs=pl.BlockSpec(memory_space=pltpu.HBM),
        scratch_shapes=[
            pltpu.VMEM((frames, channels * rows, cols), f32),
            pltpu.VMEM((taps, 3, 3, channels, channels), f32),
            pltpu.VMEM((1, channels), f32),
            pltpu.VMEM((2, taps, 3 * channels, 3 * depth), bf16),
            pltpu.VMEM((frames, rows, channels, cols), f32),
            pltpu.VMEM((frames, 2, channels, cols), f32),
            pltpu.VMEM((frames, rows + 2, 2, depth, cols), bf16),
            pltpu.VMEM((frames, 3 * channels, rows * cols), f32),
            pltpu.VMEM((frames, rows, channels, cols), f32),
            pltpu.VMEM((frames, channels * rows, cols), f32),
            pltpu.VMEM((channels, cols), f32),
            dma(()),
            dma(()),
            dma((taps, 3)),
            dma((frames, chunks)),
            dma((frames, chunks)),
            dma((frames, chunks, 2, 2)),
            dma((frames, chunks, 2)),
            dma((frames, layers)),
            dma((frames,)),
            dma((frames,)),
        ],
        compiler_params=pltpu.CompilerParams(
            collective_id=0, has_side_effects=True, vmem_limit_bytes=64 * 1024 * 1024
        ),
        cost_estimate=pl.CostEstimate(
            flops=6 * macs, bytes_accessed=4 * conv_weight.size, transcendentals=latents.size
        ),
    )(latents.reshape(frames, channels * rows, cols), conv_weight, gain)
    return out.reshape(frames, share, rows, cols)


def solution(mesh):
    return jax.shard_map(
        local,
        mesh=mesh,
        in_specs=(
            P("groups", None, "tiles", None),
            P("section", None, None, None),
            P("section", None),
        ),
        out_specs=P("groups", "section", "tiles", None),
        check_vma=False,
    )
```

```python
import functools

import jax
import jax.numpy as jnp
from jax import lax
from jax.experimental import pallas as pl
from jax.experimental.pallas import tpu as pltpu
from jax.sharding import PartitionSpec as P

EPSILON = 1e-06
MESH = pl.DeviceIdType.MESH


def halves(value):
    high = value.astype(jnp.bfloat16)
    low = (value - high.astype(jnp.float32)).astype(jnp.bfloat16)
    return high, low


def kernel(
    dims,
    lat_ref, weight_ref, gain_ref, out_ref,
    lat, raw, gain_row, weights, main, halo, normed, acc, result, stage, gain_col,
    lat_sem, gain_sem, weight_sem, main_send, main_recv, edge_send, edge_recv,
    out_send, out_recv, own_sem,
):
    frames, rows, channels, cols, layers, tiles, first_tap, chunks, depth = dims
    share = channels // layers
    part = channels // chunks
    section = lax.axis_index("section")
    tile = lax.axis_index("tiles")
    last = layers - 1
    has_up = tile > 0
    has_down = tile < tiles - 1
    taps = 3 - first_tap
    even = section % 2 == 0
    direct_out = even & (section < last)
    sides = ((has_up, -1), (has_down, 1))

    def weight_copy(a, b):
        return pltpu.make_async_copy(
            weight_ref.at[0, pl.ds(9 * (a + first_tap) + 3 * b, 3)],
            raw.at[a, b],
            weight_sem.at[a, b],
        )

    lat_copy = pltpu.make_async_copy(lat_ref, lat, lat_sem)
    gain_copy = pltpu.make_async_copy(gain_ref, gain_row, gain_sem)

    @pl.when(section == 0)
    def _():
        lat_copy.start()

    gain_copy.start()
    order = [(a, b) for a in reversed(range(taps)) for b in (1, 0, 2)]
    for a, b in order:
        weight_copy(a, b).start()

    barrier = pltpu.get_barrier_semaphore()
    links = [
        (section > 0, {"section": section - 1}),
        (section < last, {"section": section + 1}),
        (section < last, {"section": last}),
    ]
    links += [(section == last, {"section": peer}) for peer in range(last)]
    for present, step in sides:
        links.append((present & even, {"tiles": tile + step}))
        links.append((present & direct_out, {"tiles": tile + step, "section": section + 1}))
        links.append(
            (present & jnp.logical_not(even), {"tiles": tile + step, "section": section - 1})
        )

    def greet(condition, target):
        @pl.when(condition)
        def _():
            pl.semaphore_signal(barrier, inc=1, device_id=target, device_id_type=MESH)

    for condition, target in links:
        greet(condition, target)

    def piece(k):
        return pl.ds(k * part, part)

    def edge_copy(f, k, side, direct):
        source = result if direct else main
        target = {"tiles": tile + sides[side][1]}
        if direct:
            target["section"] = section + 1
        return pltpu.make_async_remote_copy(
            src_ref=source.at[f, 0 if side == 0 else rows - 1, piece(k)],
            dst_ref=halo.at[f, 1 - side, piece(k)],
            send_sem=edge_send.at[f, k, side, int(direct)],
            recv_sem=edge_recv.at[f, k, 1 - side],
            device_id=target, device_id_type=MESH,
        )

    def main_copy(f, k):
        return pltpu.make_async_remote_copy(
            src_ref=result.at[f, :, piece(k)], dst_ref=main.at[f, :, piece(k)],
            send_sem=main_send.at[f, k], recv_sem=main_recv.at[f, k],
            device_id={"section": section + 1}, device_id_type=MESH,
        )

    def out_copy(f, peer):
        return pltpu.make_async_remote_copy(
            src_ref=stage.at[f, pl.ds(peer * share * rows, share * rows)],
            dst_ref=out_ref.at[f],
            send_sem=out_send.at[f, peer], recv_sem=out_recv.at[f],
            device_id={"section": peer}, device_id_type=MESH,
        )

    def own_copy(f):
        return pltpu.make_async_copy(
            stage.at[f, pl.ds(last * share * rows, share * rows)], out_ref.at[f], own_sem.at[f]
        )

    def send_edges(f, k, direct):
        for side, (present, _) in enumerate(sides):
            @pl.when(present)
            def _():
                edge_copy(f, k, side, direct).start()

    @pl.when(section == 0)
    def _():
        lat_copy.wait()
        for f in range(frames):
            for r in range(rows):
                main[f, r] = lat[f, pl.ds(r, channels, stride=rows), :]

    for side, (present, _) in enumerate(sides):
        @pl.when(jnp.logical_not(present))
        def _():
            for f in range(frames):
                halo[f, side] = jnp.zeros((channels, cols), jnp.float32)

    pl.semaphore_wait(barrier, sum(condition.astype(jnp.int32) for condition, _ in links))

    @pl.when(section == 0)
    def _():
        for f in range(frames):
            for k in range(chunks):
                send_edges(f, k, False)

    gain_copy.wait()
    diagonal = lax.broadcasted_iota(jnp.int32, (channels, channels), 0) == (
        lax.broadcasted_iota(jnp.int32, (channels, channels), 1)
    )
    column = jnp.sum(
        jnp.where(diagonal, jnp.broadcast_to(gain_row[0:1, :], (channels, channels)), 0.0),
        axis=1, keepdims=True,
    )
    gain_col[...] = jnp.broadcast_to(column, (channels, cols))

    blank = jnp.zeros((depth - channels, cols), jnp.bfloat16)
    for f in range(frames):
        for r in range(rows + 2):
            for h in range(2):
                normed[f, r, h, pl.ds(channels, depth - channels), :] = blank

    rim = jnp.zeros((channels, depth - channels), jnp.bfloat16)
    for a, b in order:
        weight_copy(a, b).wait()
        for e in range(3):
            for h, half in enumerate(halves(raw[a, b, e])):
                half = jnp.concatenate([half, rim], axis=1)
                for k in range(chunks):
                    weights[
                        h, a, pl.ds((3 * k + e) * part, part), pl.ds(b * depth, depth)
                    ] = half[k * part : (k + 1) * part]

    def normalize(values, f, place):
        meansq = jnp.mean(values * values, axis=0, keepdims=True)
        scaled = values * lax.rsqrt(meansq + EPSILON) * gain_col[...]
        for h, half in enumerate(halves(scaled / (1.0 + jnp.exp(-scaled)))):
            normed[f, place, h, pl.ds(0, channels), :] = half

    def product(f, a, offsets, first, count):
        source = f - 2 + a + first_tap
        high, low = (
            jnp.concatenate([weights[h, a, pl.ds(first, count), pl.ds(b * depth, depth)] for b in offsets], axis=1)
            for h in range(2)
        )

        def windows(h):
            return [
                jnp.concatenate([normed[source, r + b, h] for b in offsets], axis=0)
                for r in range(rows)
            ]

        width = rows * cols
        wide = jnp.dot(
            high,
            jnp.concatenate(windows(0) + windows(1), axis=1),
            preferred_element_type=jnp.float32,
        )
        rest = jnp.dot(
            low, jnp.concatenate(windows(0), axis=1), preferred_element_type=jnp.float32
        )
        return wide[:, :width] + (wide[:, width:] + rest)

    lane = lax.broadcasted_iota(jnp.int32, (part, cols), 1)

    for f in range(frames):
        fresh = True
        for a in range(taps - 1):
            if f - 2 + a + first_tap >= 0:
                value = product(f, a, (0, 1, 2), 0, 3 * channels)
                acc[f] = value if fresh else acc[f] + value
                fresh = False

        @pl.when(section > 0)
        def _():
            for k in range(chunks):
                main_copy(f, k).wait_recv()

                @pl.when(even)
                def _():
                    send_edges(f, k, False)

        for r in range(rows):
            normalize(main[f, r], f, r + 1)
        value = product(f, taps - 1, (1,), 0, 3 * channels)
        acc[f] = value if fresh else acc[f] + value

        for side, (present, _) in enumerate(sides):
            @pl.when(present)
            def _():
                for k in range(chunks):
                    edge_copy(f, k, 1 - side, False).wait_recv()

        normalize(halo[f, 0], f, 0)
        normalize(halo[f, 1], f, rows + 1)
        for k in range(chunks):
            base = 3 * k * part
            value = acc[f, pl.ds(base, 3 * part), :] + product(
                f, taps - 1, (0, 2), base, 3 * part
            )
            for r in range(rows):
                span = slice(r * cols, (r + 1) * cols)
                before = pltpu.roll(value[:part, span], 1, 1)
                after = pltpu.roll(value[2 * part :, span], cols - 1, 1)
                result[f, r, piece(k)] = (
                    main[f, r, piece(k)]
                    + value[part : 2 * part, span]
                    + jnp.where(lane > 0, before, 0.0)
                    + jnp.where(lane < cols - 1, after, 0.0)
                )

            @pl.when(section < last)
            def _():
                @pl.when(even)
                def _():
                    send_edges(f, k, True)

                main_copy(f, k).start()

            @pl.when(section == last)
            def _():
                for r in range(rows):
                    stage[f, pl.ds(k * part * rows + r, part, stride=rows), :] = result[
                        f, r, piece(k)
                    ]
                for peer in range(k * layers // chunks, (k + 1) * layers // chunks):
                    if peer < last:
                        out_copy(f, peer).start()
                    else:
                        own_copy(f).start()

    for f in range(frames):
        for k in range(chunks):
            for side, (present, _) in enumerate(sides):
                @pl.when(present & even)
                def _():
                    edge_copy(f, k, side, False).wait_send()

                @pl.when(present & direct_out)
                def _():
                    edge_copy(f, k, side, True).wait_send()

            @pl.when(section < last)
            def _():
                main_copy(f, k).wait_send()

        @pl.when(section == last)
        def _():
            for peer in range(last):
                out_copy(f, peer).wait_send()
            own_copy(f).wait()

    @pl.when(section < last)
    def _():
        for f in range(frames):
            out_copy(f, 0).wait_recv()


def local(latents, conv_weight, gain):
    frames, channels, rows, cols = latents.shape
    layers = lax.axis_size("section")
    tiles = lax.axis_size("tiles")
    share = channels // layers
    first_tap = max(0, 3 - frames)
    taps = 3 - first_tap
    chunks = 2
    depth = -(-channels // 256) * 256
    f32, bf16 = jnp.float32, jnp.bfloat16
    dma = pltpu.SemaphoreType.DMA
    macs = frames * rows * cols * channels * channels * 27
    dims = (frames, rows, channels, cols, layers, tiles, first_tap, chunks, depth)
    out = pl.pallas_call(
        functools.partial(kernel, dims),
        out_shape=jax.ShapeDtypeStruct((frames, share * rows, cols), f32),
        in_specs=[pl.BlockSpec(memory_space=pltpu.HBM)] * 3,
        out_specs=pl.BlockSpec(memory_space=pltpu.HBM),
        scratch_shapes=[
            pltpu.VMEM((frames, channels * rows, cols), f32),
            pltpu.VMEM((taps, 3, 3, channels, channels), f32),
            pltpu.VMEM((1, channels), f32),
            pltpu.VMEM((2, taps, 3 * channels, 3 * depth), bf16),
            pltpu.VMEM((frames, rows, channels, cols), f32),
            pltpu.VMEM((frames, 2, channels, cols), f32),
            pltpu.VMEM((frames, rows + 2, 2, depth, cols), bf16),
            pltpu.VMEM((frames, 3 * channels, rows * cols), f32),
            pltpu.VMEM((frames, rows, channels, cols), f32),
            pltpu.VMEM((frames, channels * rows, cols), f32),
            pltpu.VMEM((channels, cols), f32),
            dma(()),
            dma(()),
            dma((taps, 3)),
            dma((frames, chunks)),
            dma((frames, chunks)),
            dma((frames, chunks, 2, 2)),
            dma((frames, chunks, 2)),
            dma((frames, layers)),
            dma((frames,)),
            dma((frames,)),
        ],
        compiler_params=pltpu.CompilerParams(
            collective_id=0, has_side_effects=True, vmem_limit_bytes=64 * 1024 * 1024
        ),
        cost_estimate=pl.CostEstimate(
            flops=6 * macs, bytes_accessed=4 * conv_weight.size, transcendentals=latents.size
        ),
    )(latents.reshape(frames, channels * rows, cols), conv_weight, gain)
    return out.reshape(frames, share, rows, cols)


def solution(mesh):
    return jax.shard_map(
        local,
        mesh=mesh,
        in_specs=(
            P("groups", None, "tiles", None),
            P("section", None, None, None),
            P("section", None),
        ),
        out_specs=P("groups", "section", "tiles", None),
        check_vma=False,
    )
```

```python
import functools

import jax
import jax.numpy as jnp
from jax import lax
from jax.experimental import pallas as pl
from jax.experimental.pallas import tpu as pltpu
from jax.sharding import PartitionSpec as P

EPSILON = 1e-06
MESH = pl.DeviceIdType.MESH


def halves(value):
    high = value.astype(jnp.bfloat16)
    low = (value - high.astype(jnp.float32)).astype(jnp.bfloat16)
    return high, low


def kernel(
    dims,
    lat_ref, weight_ref, gain_ref, out_ref,
    lat, raw, gain_row, weights, main, halo, normed, acc, result, stage, gain_col,
    lat_sem, gain_sem, weight_sem, main_send, main_recv, edge_send, edge_recv,
    out_send, out_recv, own_sem,
):
    frames, rows, channels, cols, layers, tiles, first_tap, chunks, depth = dims
    share = channels // layers
    part = channels // chunks
    section = lax.axis_index("section")
    tile = lax.axis_index("tiles")
    last = layers - 1
    has_up = tile > 0
    has_down = tile < tiles - 1
    taps = 3 - first_tap
    even = section % 2 == 0
    sends_on = section < last
    sides = ((has_up, -1), (has_down, 1))

    def weight_copy(a, b):
        return pltpu.make_async_copy(
            weight_ref.at[0, pl.ds(9 * (a + first_tap) + 3 * b, 3)],
            raw.at[a, b],
            weight_sem.at[a, b],
        )

    lat_copy = pltpu.make_async_copy(lat_ref, lat, lat_sem)
    gain_copy = pltpu.make_async_copy(gain_ref, gain_row, gain_sem)

    @pl.when(section == 0)
    def _():
        lat_copy.start()

    gain_copy.start()
    order = [(a, b) for a in reversed(range(taps)) for b in (1, 0, 2)]
    for a, b in order:
        weight_copy(a, b).start()

    barrier = pltpu.get_barrier_semaphore()
    links = [
        (section > 0, {"section": section - 1}),
        (section < last, {"section": section + 1}),
        (section < last, {"section": last}),
    ]
    links += [(section == last, {"section": peer}) for peer in range(last)]
    for present, step in sides:
        links.append((present & even, {"tiles": tile + step}))
        links.append((present & sends_on, {"tiles": tile + step, "section": section + 1}))
        links.append((present & (section > 0), {"tiles": tile + step, "section": section - 1}))

    def greet(condition, target):
        @pl.when(condition)
        def _():
            pl.semaphore_signal(barrier, inc=1, device_id=target, device_id_type=MESH)

    for condition, target in links:
        greet(condition, target)

    def piece(k):
        return pl.ds(k * part, part)

    def edge_copy(f, k, side, direct):
        source = result if direct else main
        target = {"tiles": tile + sides[side][1]}
        if direct:
            target["section"] = section + 1
        return pltpu.make_async_remote_copy(
            src_ref=source.at[f, 0 if side == 0 else rows - 1, piece(k)],
            dst_ref=halo.at[f, 1 - side, piece(k)],
            send_sem=edge_send.at[f, k, side, int(direct)],
            recv_sem=edge_recv.at[f, k, 1 - side],
            device_id=target, device_id_type=MESH,
        )

    def main_copy(f, k):
        return pltpu.make_async_remote_copy(
            src_ref=result.at[f, :, piece(k)], dst_ref=main.at[f, :, piece(k)],
            send_sem=main_send.at[f, k], recv_sem=main_recv.at[f, k],
            device_id={"section": section + 1}, device_id_type=MESH,
        )

    def out_copy(f, peer):
        return pltpu.make_async_remote_copy(
            src_ref=stage.at[f, pl.ds(peer * share * rows, share * rows)],
            dst_ref=out_ref.at[f],
            send_sem=out_send.at[f, peer], recv_sem=out_recv.at[f],
            device_id={"section": peer}, device_id_type=MESH,
        )

    def own_copy(f):
        return pltpu.make_async_copy(
            stage.at[f, pl.ds(last * share * rows, share * rows)], out_ref.at[f], own_sem.at[f]
        )

    def send_edges(f, k, direct):
        for side, (present, _) in enumerate(sides):
            @pl.when(present)
            def _():
                edge_copy(f, k, side, direct).start()

    @pl.when(section == 0)
    def _():
        lat_copy.wait()
        for f in range(frames):
            for r in range(rows):
                main[f, r] = lat[f, pl.ds(r, channels, stride=rows), :]

    for side, (present, _) in enumerate(sides):
        @pl.when(jnp.logical_not(present))
        def _():
            for f in range(frames):
                halo[f, side] = jnp.zeros((channels, cols), jnp.float32)

    pl.semaphore_wait(barrier, sum(condition.astype(jnp.int32) for condition, _ in links))

    @pl.when(section == 0)
    def _():
        for f in range(frames):
            for k in range(chunks):
                send_edges(f, k, False)

    gain_copy.wait()
    diagonal = lax.broadcasted_iota(jnp.int32, (channels, channels), 0) == (
        lax.broadcasted_iota(jnp.int32, (channels, channels), 1)
    )
    column = jnp.sum(
        jnp.where(diagonal, jnp.broadcast_to(gain_row[0:1, :], (channels, channels)), 0.0),
        axis=1, keepdims=True,
    )
    gain_col[...] = jnp.broadcast_to(column, (channels, cols))

    blank = jnp.zeros((depth - channels, cols), jnp.bfloat16)
    for f in range(frames):
        for r in range(rows + 2):
            for h in range(2):
                normed[f, r, h, pl.ds(channels, depth - channels), :] = blank

    rim = jnp.zeros((channels, depth - channels), jnp.bfloat16)
    for a, b in order:
        weight_copy(a, b).wait()
        for e in range(3):
            for h, half in enumerate(halves(raw[a, b, e])):
                half = jnp.concatenate([half, rim], axis=1)
                for k in range(chunks):
                    weights[
                        h, a, pl.ds((3 * k + e) * part, part), pl.ds(b * depth, depth)
                    ] = half[k * part : (k + 1) * part]

    def normalize(values, f, place):
        meansq = jnp.mean(values * values, axis=0, keepdims=True)
        scaled = values * lax.rsqrt(meansq + EPSILON) * gain_col[...]
        for h, half in enumerate(halves(scaled / (1.0 + jnp.exp(-scaled)))):
            normed[f, place, h, pl.ds(0, channels), :] = half

    def product(f, a, offsets, first, count):
        source = f - 2 + a + first_tap
        high, low = (
            jnp.concatenate([weights[h, a, pl.ds(first, count), pl.ds(b * depth, depth)] for b in offsets], axis=1)
            for h in range(2)
        )

        def windows(h):
            return [
                jnp.concatenate([normed[source, r + b, h] for b in offsets], axis=0)
                for r in range(rows)
            ]

        width = rows * cols
        wide = jnp.dot(
            high,
            jnp.concatenate(windows(0) + windows(1), axis=1),
            preferred_element_type=jnp.float32,
        )
        rest = jnp.dot(
            low, jnp.concatenate(windows(0), axis=1), preferred_element_type=jnp.float32
        )
        return wide[:, :width] + (wide[:, width:] + rest)

    lane = lax.broadcasted_iota(jnp.int32, (part, cols), 1)

    for f in range(frames):
        fresh = True
        for a in range(taps - 1):
            if f - 2 + a + first_tap >= 0:
                value = product(f, a, (0, 1, 2), 0, 3 * channels)
                acc[f] = value if fresh else acc[f] + value
                fresh = False

        @pl.when(section > 0)
        def _():
            for k in range(chunks):
                main_copy(f, k).wait_recv()
                if k < chunks - 1:
                    @pl.when(even)
                    def _():
                        send_edges(f, k, False)

        for r in range(rows):
            normalize(main[f, r], f, r + 1)
        value = product(f, taps - 1, (1,), 0, 3 * channels)
        acc[f] = value if fresh else acc[f] + value

        for side, (present, _) in enumerate(sides):
            @pl.when(present)
            def _():
                for k in range(chunks):
                    edge_copy(f, k, 1 - side, False).wait_recv()

        normalize(halo[f, 0], f, 0)
        normalize(halo[f, 1], f, rows + 1)
        for k in range(chunks):
            base = 3 * k * part
            value = acc[f, pl.ds(base, 3 * part), :] + product(
                f, taps - 1, (0, 2), base, 3 * part
            )
            for r in range(rows):
                span = slice(r * cols, (r + 1) * cols)
                before = pltpu.roll(value[:part, span], 1, 1)
                after = pltpu.roll(value[2 * part :, span], cols - 1, 1)
                result[f, r, piece(k)] = (
                    main[f, r, piece(k)]
                    + value[part : 2 * part, span]
                    + jnp.where(lane > 0, before, 0.0)
                    + jnp.where(lane < cols - 1, after, 0.0)
                )

            @pl.when(section < last)
            def _():
                main_copy(f, k).start()
                if k < chunks - 1:
                    @pl.when(even)
                    def _():
                        send_edges(f, k, True)
                else:
                    send_edges(f, k, True)

            @pl.when(section == last)
            def _():
                for r in range(rows):
                    stage[f, pl.ds(k * part * rows + r, part, stride=rows), :] = result[
                        f, r, piece(k)
                    ]
                for peer in range(k * layers // chunks, (k + 1) * layers // chunks):
                    if peer < last:
                        out_copy(f, peer).start()
                    else:
                        own_copy(f).start()

    for f in range(frames):
        for k in range(chunks):
            for side, (present, _) in enumerate(sides):
                whole = k == chunks - 1

                @pl.when(present & ((section == 0) if whole else even))
                def _():
                    edge_copy(f, k, side, False).wait_send()

                @pl.when(present & (sends_on if whole else sends_on & even))
                def _():
                    edge_copy(f, k, side, True).wait_send()

            @pl.when(section < last)
            def _():
                main_copy(f, k).wait_send()

        @pl.when(section == last)
        def _():
            for peer in range(last):
                out_copy(f, peer).wait_send()
            own_copy(f).wait()

    @pl.when(section < last)
    def _():
        for f in range(frames):
            out_copy(f, 0).wait_recv()


def local(latents, conv_weight, gain):
    frames, channels, rows, cols = latents.shape
    layers = lax.axis_size("section")
    tiles = lax.axis_size("tiles")
    share = channels // layers
    first_tap = max(0, 3 - frames)
    taps = 3 - first_tap
    chunks = 2
    depth = -(-channels // 256) * 256
    f32, bf16 = jnp.float32, jnp.bfloat16
    dma = pltpu.SemaphoreType.DMA
    macs = frames * rows * cols * channels * channels * 27
    dims = (frames, rows, channels, cols, layers, tiles, first_tap, chunks, depth)
    out = pl.pallas_call(
        functools.partial(kernel, dims),
        out_shape=jax.ShapeDtypeStruct((frames, share * rows, cols), f32),
        in_specs=[pl.BlockSpec(memory_space=pltpu.HBM)] * 3,
        out_specs=pl.BlockSpec(memory_space=pltpu.HBM),
        scratch_shapes=[
            pltpu.VMEM((frames, channels * rows, cols), f32),
            pltpu.VMEM((taps, 3, 3, channels, channels), f32),
            pltpu.VMEM((1, channels), f32),
            pltpu.VMEM((2, taps, 3 * channels, 3 * depth), bf16),
            pltpu.VMEM((frames, rows, channels, cols), f32),
            pltpu.VMEM((frames, 2, channels, cols), f32),
            pltpu.VMEM((frames, rows + 2, 2, depth, cols), bf16),
            pltpu.VMEM((frames, 3 * channels, rows * cols), f32),
            pltpu.VMEM((frames, rows, channels, cols), f32),
            pltpu.VMEM((frames, channels * rows, cols), f32),
            pltpu.VMEM((channels, cols), f32),
            dma(()),
            dma(()),
            dma((taps, 3)),
            dma((frames, chunks)),
            dma((frames, chunks)),
            dma((frames, chunks, 2, 2)),
            dma((frames, chunks, 2)),
            dma((frames, layers)),
            dma((frames,)),
            dma((frames,)),
        ],
        compiler_params=pltpu.CompilerParams(
            collective_id=0, has_side_effects=True, vmem_limit_bytes=64 * 1024 * 1024
        ),
        cost_estimate=pl.CostEstimate(
            flops=6 * macs, bytes_accessed=4 * conv_weight.size, transcendentals=latents.size
        ),
    )(latents.reshape(frames, channels * rows, cols), conv_weight, gain)
    return out.reshape(frames, share, rows, cols)


def solution(mesh):
    return jax.shard_map(
        local,
        mesh=mesh,
        in_specs=(
            P("groups", None, "tiles", None),
            P("section", None, None, None),
            P("section", None),
        ),
        out_specs=P("groups", "section", "tiles", None),
        check_vma=False,
    )
```

```python
import functools

import jax
import jax.numpy as jnp
from jax import lax
from jax.experimental import pallas as pl
from jax.experimental.pallas import tpu as pltpu
from jax.sharding import PartitionSpec as P

EPSILON = 1e-06
MESH = pl.DeviceIdType.MESH


def halves(value):
    high = value.astype(jnp.bfloat16)
    low = (value - high.astype(jnp.float32)).astype(jnp.bfloat16)
    return high, low


def kernel(
    dims,
    lat_ref, weight_ref, gain_ref, out_ref,
    lat, raw, gain_row, weights, main, halo, normed, acc, result, stage, gain_col,
    lat_sem, gain_sem, weight_sem, main_send, main_recv, edge_send, edge_recv,
    out_send, out_recv, own_sem,
):
    frames, rows, channels, cols, layers, tiles, first_tap, chunks, depth = dims
    share = channels // layers
    part = channels // chunks
    section = lax.axis_index("section")
    tile = lax.axis_index("tiles")
    last = layers - 1
    has_up = tile > 0
    has_down = tile < tiles - 1
    taps = 3 - first_tap
    even = section % 2 == 0
    sends_on = section < last
    sides = ((has_up, -1), (has_down, 1))

    def weight_copy(a, b):
        return pltpu.make_async_copy(
            weight_ref.at[0, pl.ds(9 * (a + first_tap) + 3 * b, 3)],
            raw.at[a, b],
            weight_sem.at[a, b],
        )

    lat_copy = pltpu.make_async_copy(lat_ref, lat, lat_sem)
    gain_copy = pltpu.make_async_copy(gain_ref, gain_row, gain_sem)

    @pl.when(section == 0)
    def _():
        lat_copy.start()

    gain_copy.start()
    order = [(a, b) for a in reversed(range(taps)) for b in (1, 0, 2)]
    for a, b in order:
        weight_copy(a, b).start()

    barrier = pltpu.get_barrier_semaphore()
    links = [
        (section > 0, {"section": section - 1}),
        (section < last, {"section": section + 1}),
        (section < last, {"section": last}),
    ]
    links += [(section == last, {"section": peer}) for peer in range(last)]
    for present, step in sides:
        links.append((present & even, {"tiles": tile + step}))
        links.append((present & sends_on, {"tiles": tile + step, "section": section + 1}))
        links.append((present & (section > 0), {"tiles": tile + step, "section": section - 1}))

    def greet(condition, target):
        @pl.when(condition)
        def _():
            pl.semaphore_signal(barrier, inc=1, device_id=target, device_id_type=MESH)

    for condition, target in links:
        greet(condition, target)

    def piece(k):
        return pl.ds(k * part, part)

    def edge_copy(f, k, side, direct):
        source = result if direct else main
        target = {"tiles": tile + sides[side][1]}
        if direct:
            target["section"] = section + 1
        return pltpu.make_async_remote_copy(
            src_ref=source.at[f, 0 if side == 0 else rows - 1, piece(k)],
            dst_ref=halo.at[f, 1 - side, piece(k)],
            send_sem=edge_send.at[f, k, side, int(direct)],
            recv_sem=edge_recv.at[f, k, 1 - side],
            device_id=target, device_id_type=MESH,
        )

    def main_copy(f, k):
        return pltpu.make_async_remote_copy(
            src_ref=result.at[f, :, piece(k)], dst_ref=main.at[f, :, piece(k)],
            send_sem=main_send.at[f, k], recv_sem=main_recv.at[f, k],
            device_id={"section": section + 1}, device_id_type=MESH,
        )

    def out_copy(f, peer):
        return pltpu.make_async_remote_copy(
            src_ref=stage.at[f, pl.ds(peer * share * rows, share * rows)],
            dst_ref=out_ref.at[f],
            send_sem=out_send.at[f, peer], recv_sem=out_recv.at[f],
            device_id={"section": peer}, device_id_type=MESH,
        )

    def own_copy(f):
        return pltpu.make_async_copy(
            stage.at[f, pl.ds(last * share * rows, share * rows)], out_ref.at[f], own_sem.at[f]
        )

    def send_edges(f, k, direct):
        for side, (present, _) in enumerate(sides):
            @pl.when(present)
            def _():
                edge_copy(f, k, side, direct).start()

    @pl.when(section == 0)
    def _():
        lat_copy.wait()
        for f in range(frames):
            for r in range(rows):
                main[f, r] = lat[f, pl.ds(r, channels, stride=rows), :]

    for side, (present, _) in enumerate(sides):
        @pl.when(jnp.logical_not(present))
        def _():
            for f in range(frames):
                halo[f, side] = jnp.zeros((channels, cols), jnp.float32)

    pl.semaphore_wait(barrier, sum(condition.astype(jnp.int32) for condition, _ in links))

    @pl.when(section == 0)
    def _():
        for f in range(frames):
            for k in range(chunks):
                send_edges(f, k, False)

    gain_copy.wait()
    diagonal = lax.broadcasted_iota(jnp.int32, (channels, channels), 0) == (
        lax.broadcasted_iota(jnp.int32, (channels, channels), 1)
    )
    column = jnp.sum(
        jnp.where(diagonal, jnp.broadcast_to(gain_row[0:1, :], (channels, channels)), 0.0),
        axis=1, keepdims=True,
    )
    gain_col[...] = jnp.broadcast_to(column, (channels, cols))

    blank = jnp.zeros((depth - channels, cols), jnp.bfloat16)
    for f in range(frames):
        for r in range(rows + 2):
            for h in range(2):
                normed[f, r, h, pl.ds(channels, depth - channels), :] = blank

    rim = jnp.zeros((channels, depth - channels), jnp.bfloat16)
    for a, b in order:
        weight_copy(a, b).wait()
        for e in range(3):
            for h, half in enumerate(halves(raw[a, b, e])):
                half = jnp.concatenate([half, rim], axis=1)
                for k in range(chunks):
                    weights[
                        h, a, pl.ds((3 * k + e) * part, part), pl.ds(b * depth, depth)
                    ] = half[k * part : (k + 1) * part]

    def normalize(values, f, place):
        meansq = jnp.mean(values * values, axis=0, keepdims=True)
        scaled = values * lax.rsqrt(meansq + EPSILON) * gain_col[...]
        for h, half in enumerate(halves(scaled / (1.0 + jnp.exp(-scaled)))):
            normed[f, place, h, pl.ds(0, channels), :] = half

    def product(f, a, offsets, first, count):
        source = f - 2 + a + first_tap
        high, low = (
            jnp.concatenate([weights[h, a, pl.ds(first, count), pl.ds(b * depth, depth)] for b in offsets], axis=1)
            for h in range(2)
        )

        def windows(h):
            return [
                jnp.concatenate([normed[source, r + b, h] for b in offsets], axis=0)
                for r in range(rows)
            ]

        width = rows * cols
        wide = jnp.dot(
            high,
            jnp.concatenate(windows(0) + windows(1), axis=1),
            preferred_element_type=jnp.float32,
        )
        rest = jnp.dot(
            low, jnp.concatenate(windows(0), axis=1), preferred_element_type=jnp.float32
        )
        return wide[:, :width] + (wide[:, width:] + rest)

    lane = lax.broadcasted_iota(jnp.int32, (part, cols), 1)

    for f in range(frames):
        fresh = True
        for a in range(taps - 1):
            if f - 2 + a + first_tap >= 0:
                value = product(f, a, (0, 1, 2), 0, 3 * channels)
                acc[f] = value if fresh else acc[f] + value
                fresh = False

        @pl.when(section > 0)
        def _():
            for k in range(chunks):
                main_copy(f, k).wait_recv()
                if k < chunks - 1:
                    @pl.when(even)
                    def _():
                        send_edges(f, k, False)

        for r in range(rows):
            normalize(main[f, r], f, r + 1)
        value = product(f, taps - 1, (1,), 0, 3 * channels)
        acc[f] = value if fresh else acc[f] + value

        for side, (present, _) in enumerate(sides):
            @pl.when(present)
            def _():
                for k in range(chunks):
                    edge_copy(f, k, 1 - side, False).wait_recv()

        normalize(halo[f, 0], f, 0)
        normalize(halo[f, 1], f, rows + 1)
        for k in range(chunks):
            base = 3 * k * part
            value = acc[f, pl.ds(base, 3 * part), :] + product(
                f, taps - 1, (0, 2), base, 3 * part
            )
            for r in range(rows):
                span = slice(r * cols, (r + 1) * cols)
                before = pltpu.roll(value[:part, span], 1, 1)
                after = pltpu.roll(value[2 * part :, span], cols - 1, 1)
                result[f, r, piece(k)] = (
                    main[f, r, piece(k)]
                    + value[part : 2 * part, span]
                    + jnp.where(lane > 0, before, 0.0)
                    + jnp.where(lane < cols - 1, after, 0.0)
                )

            @pl.when(section < last)
            def _():
                main_copy(f, k).start()
                if k < chunks - 1:
                    @pl.when(even)
                    def _():
                        send_edges(f, k, True)
                else:
                    send_edges(f, k, True)

            @pl.when(section == last)
            def _():
                for r in range(rows):
                    stage[f, pl.ds(k * part * rows + r, part, stride=rows), :] = result[
                        f, r, piece(k)
                    ]
                for peer in range(k * layers // chunks, (k + 1) * layers // chunks):
                    if peer < last:
                        out_copy(f, peer).start()
                    else:
                        own_copy(f).start()

    for f in range(frames):
        for k in range(chunks):
            for side, (present, _) in enumerate(sides):
                whole = k == chunks - 1

                @pl.when(present & ((section == 0) if whole else even))
                def _():
                    edge_copy(f, k, side, False).wait_send()

                @pl.when(present & (sends_on if whole else sends_on & even))
                def _():
                    edge_copy(f, k, side, True).wait_send()

            @pl.when(section < last)
            def _():
                main_copy(f, k).wait_send()

        @pl.when(section == last)
        def _():
            for peer in range(last):
                out_copy(f, peer).wait_send()
            own_copy(f).wait()

    @pl.when(section < last)
    def _():
        for f in range(frames):
            out_copy(f, 0).wait_recv()


def local(latents, conv_weight, gain):
    frames, channels, rows, cols = latents.shape
    layers = lax.axis_size("section")
    tiles = lax.axis_size("tiles")
    share = channels // layers
    first_tap = max(0, 3 - frames)
    taps = 3 - first_tap
    chunks = 4
    depth = -(-channels // 256) * 256
    f32, bf16 = jnp.float32, jnp.bfloat16
    dma = pltpu.SemaphoreType.DMA
    macs = frames * rows * cols * channels * channels * 27
    dims = (frames, rows, channels, cols, layers, tiles, first_tap, chunks, depth)
    out = pl.pallas_call(
        functools.partial(kernel, dims),
        out_shape=jax.ShapeDtypeStruct((frames, share * rows, cols), f32),
        in_specs=[pl.BlockSpec(memory_space=pltpu.HBM)] * 3,
        out_specs=pl.BlockSpec(memory_space=pltpu.HBM),
        scratch_shapes=[
            pltpu.VMEM((frames, channels * rows, cols), f32),
            pltpu.VMEM((taps, 3, 3, channels, channels), f32),
            pltpu.VMEM((1, channels), f32),
            pltpu.VMEM((2, taps, 3 * channels, 3 * depth), bf16),
            pltpu.VMEM((frames, rows, channels, cols), f32),
            pltpu.VMEM((frames, 2, channels, cols), f32),
            pltpu.VMEM((frames, rows + 2, 2, depth, cols), bf16),
            pltpu.VMEM((frames, 3 * channels, rows * cols), f32),
            pltpu.VMEM((frames, rows, channels, cols), f32),
            pltpu.VMEM((frames, channels * rows, cols), f32),
            pltpu.VMEM((channels, cols), f32),
            dma(()),
            dma(()),
            dma((taps, 3)),
            dma((frames, chunks)),
            dma((frames, chunks)),
            dma((frames, chunks, 2, 2)),
            dma((frames, chunks, 2)),
            dma((frames, layers)),
            dma((frames,)),
            dma((frames,)),
        ],
        compiler_params=pltpu.CompilerParams(
            collective_id=0, has_side_effects=True, vmem_limit_bytes=64 * 1024 * 1024
        ),
        cost_estimate=pl.CostEstimate(
            flops=6 * macs, bytes_accessed=4 * conv_weight.size, transcendentals=latents.size
        ),
    )(latents.reshape(frames, channels * rows, cols), conv_weight, gain)
    return out.reshape(frames, share, rows, cols)


def solution(mesh):
    return jax.shard_map(
        local,
        mesh=mesh,
        in_specs=(
            P("groups", None, "tiles", None),
            P("section", None, None, None),
            P("section", None),
        ),
        out_specs=P("groups", "section", "tiles", None),
        check_vma=False,
    )
```

```python
import functools

import jax
import jax.numpy as jnp
from jax import lax
from jax.experimental import pallas as pl
from jax.experimental.pallas import tpu as pltpu
from jax.sharding import PartitionSpec as P

EPSILON = 1e-06
MESH = pl.DeviceIdType.MESH


def halves(value):
    high = value.astype(jnp.bfloat16)
    low = (value - high.astype(jnp.float32)).astype(jnp.bfloat16)
    return high, low


def kernel(
    dims,
    lat_ref, weight_ref, gain_ref, out_ref,
    lat, raw, gain_row, weights, main, halo, normed, acc, result, stage, gain_col,
    lat_sem, gain_sem, weight_sem, main_send, main_recv, edge_send, edge_recv,
    out_send, out_recv, own_sem,
):
    frames, rows, channels, cols, layers, tiles, first_tap, chunks, depth = dims
    share = channels // layers
    part = channels // chunks
    section = lax.axis_index("section")
    tile = lax.axis_index("tiles")
    last = layers - 1
    has_up = tile > 0
    has_down = tile < tiles - 1
    taps = 3 - first_tap
    even = section % 2 == 0
    sends_on = section < last
    sides = ((has_up, -1), (has_down, 1))

    def weight_copy(a, b):
        return pltpu.make_async_copy(
            weight_ref.at[0, pl.ds(9 * (a + first_tap) + 3 * b, 3)],
            raw.at[a, b],
            weight_sem.at[a, b],
        )

    lat_copy = pltpu.make_async_copy(lat_ref, lat, lat_sem)
    gain_copy = pltpu.make_async_copy(gain_ref, gain_row, gain_sem)

    @pl.when(section == 0)
    def _():
        lat_copy.start()

    gain_copy.start()
    order = [(a, b) for a in reversed(range(taps)) for b in (1, 0, 2)]
    for a, b in order:
        weight_copy(a, b).start()

    barrier = pltpu.get_barrier_semaphore()
    links = [
        (section > 0, {"section": section - 1}),
        (section < last, {"section": section + 1}),
        (section < last, {"section": last}),
    ]
    links += [(section == last, {"section": peer}) for peer in range(last)]
    for present, step in sides:
        links.append((present & even, {"tiles": tile + step}))
        links.append((present & sends_on, {"tiles": tile + step, "section": section + 1}))
        links.append((present & (section > 0), {"tiles": tile + step, "section": section - 1}))

    def greet(condition, target):
        @pl.when(condition)
        def _():
            pl.semaphore_signal(barrier, inc=1, device_id=target, device_id_type=MESH)

    for condition, target in links:
        greet(condition, target)

    def piece(k):
        return pl.ds(k * part, part)

    def edge_copy(f, k, side, direct):
        source = result if direct else main
        target = {"tiles": tile + sides[side][1]}
        if direct:
            target["section"] = section + 1
        return pltpu.make_async_remote_copy(
            src_ref=source.at[f, 0 if side == 0 else rows - 1, piece(k)],
            dst_ref=halo.at[f, 1 - side, piece(k)],
            send_sem=edge_send.at[f, k, side, int(direct)],
            recv_sem=edge_recv.at[f, k, 1 - side],
            device_id=target, device_id_type=MESH,
        )

    def main_copy(f, k):
        return pltpu.make_async_remote_copy(
            src_ref=result.at[f, :, piece(k)], dst_ref=main.at[f, :, piece(k)],
            send_sem=main_send.at[f, k], recv_sem=main_recv.at[f, k],
            device_id={"section": section + 1}, device_id_type=MESH,
        )

    def out_copy(f, peer):
        return pltpu.make_async_remote_copy(
            src_ref=stage.at[f, pl.ds(peer * share * rows, share * rows)],
            dst_ref=out_ref.at[f],
            send_sem=out_send.at[f, peer], recv_sem=out_recv.at[f],
            device_id={"section": peer}, device_id_type=MESH,
        )

    def own_copy(f):
        return pltpu.make_async_copy(
            stage.at[f, pl.ds(last * share * rows, share * rows)], out_ref.at[f], own_sem.at[f]
        )

    def send_edges(f, k, direct):
        for side, (present, _) in enumerate(sides):
            @pl.when(present)
            def _():
                edge_copy(f, k, side, direct).start()

    @pl.when(section == 0)
    def _():
        lat_copy.wait()
        for f in range(frames):
            for r in range(rows):
                main[f, r] = lat[f, pl.ds(r, channels, stride=rows), :]

    for side, (present, _) in enumerate(sides):
        @pl.when(jnp.logical_not(present))
        def _():
            for f in range(frames):
                halo[f, side] = jnp.zeros((channels, cols), jnp.float32)

    pl.semaphore_wait(barrier, sum(condition.astype(jnp.int32) for condition, _ in links))

    @pl.when(section == 0)
    def _():
        for f in range(frames):
            for k in range(chunks):
                send_edges(f, k, False)

    gain_copy.wait()
    diagonal = lax.broadcasted_iota(jnp.int32, (channels, channels), 0) == (
        lax.broadcasted_iota(jnp.int32, (channels, channels), 1)
    )
    column = jnp.sum(
        jnp.where(diagonal, jnp.broadcast_to(gain_row[0:1, :], (channels, channels)), 0.0),
        axis=1, keepdims=True,
    )
    gain_col[...] = jnp.broadcast_to(column, (channels, cols))

    blank = jnp.zeros((depth - channels, cols), jnp.bfloat16)
    for f in range(frames):
        for r in range(rows + 2):
            for h in range(2):
                normed[f, r, h, pl.ds(channels, depth - channels), :] = blank

    rim = jnp.zeros((channels, depth - channels), jnp.bfloat16)
    for a, b in order:
        weight_copy(a, b).wait()
        for e in range(3):
            for h, half in enumerate(halves(raw[a, b, e])):
                half = jnp.concatenate([half, rim], axis=1)
                for k in range(chunks):
                    weights[
                        h, a, pl.ds((3 * k + e) * part, part), pl.ds(b * depth, depth)
                    ] = half[k * part : (k + 1) * part]

    def normalize(values, f, place):
        meansq = jnp.mean(values * values, axis=0, keepdims=True)
        scaled = values * lax.rsqrt(meansq + EPSILON) * gain_col[...]
        for h, half in enumerate(halves(scaled / (1.0 + jnp.exp(-scaled)))):
            normed[f, place, h, pl.ds(0, channels), :] = half

    def product(f, a, offsets, first, count):
        source = f - 2 + a + first_tap
        high, low = (
            jnp.concatenate([weights[h, a, pl.ds(first, count), pl.ds(b * depth, depth)] for b in offsets], axis=1)
            for h in range(2)
        )

        def windows(h):
            return [
                jnp.concatenate([normed[source, r + b, h] for b in offsets], axis=0)
                for r in range(rows)
            ]

        width = rows * cols
        wide = jnp.dot(
            high,
            jnp.concatenate(windows(0) + windows(1), axis=1),
            preferred_element_type=jnp.float32,
        )
        rest = jnp.dot(
            low, jnp.concatenate(windows(0), axis=1), preferred_element_type=jnp.float32
        )
        return wide[:, :width] + (wide[:, width:] + rest)

    lane = lax.broadcasted_iota(jnp.int32, (part, cols), 1)

    for f in range(frames):
        fresh = True
        for a in range(taps - 1):
            if f - 2 + a + first_tap >= 0:
                value = product(f, a, (0, 1, 2), 0, 3 * channels)
                acc[f] = value if fresh else acc[f] + value
                fresh = False

        @pl.when(section > 0)
        def _():
            for k in range(chunks):
                main_copy(f, k).wait_recv()
                if k < chunks - 1:
                    @pl.when(even)
                    def _():
                        send_edges(f, k, False)

        for r in range(rows):
            normalize(main[f, r], f, r + 1)
        split = f == frames - 1
        if split:
            value = product(f, taps - 1, (1,), 0, 3 * channels)
            acc[f] = value if fresh else acc[f] + value

        for side, (present, _) in enumerate(sides):
            @pl.when(present)
            def _():
                for k in range(chunks):
                    edge_copy(f, k, 1 - side, False).wait_recv()

        normalize(halo[f, 0], f, 0)
        normalize(halo[f, 1], f, rows + 1)
        if not split:
            value = product(f, taps - 1, (0, 1, 2), 0, 3 * channels)
            acc[f] = value if fresh else acc[f] + value
        for k in range(chunks):
            base = 3 * k * part
            value = acc[f, pl.ds(base, 3 * part), :]
            if split:
                value += product(f, taps - 1, (0, 2), base, 3 * part)
            for r in range(rows):
                span = slice(r * cols, (r + 1) * cols)
                before = pltpu.roll(value[:part, span], 1, 1)
                after = pltpu.roll(value[2 * part :, span], cols - 1, 1)
                result[f, r, piece(k)] = (
                    main[f, r, piece(k)]
                    + value[part : 2 * part, span]
                    + jnp.where(lane > 0, before, 0.0)
                    + jnp.where(lane < cols - 1, after, 0.0)
                )

            @pl.when(section < last)
            def _():
                main_copy(f, k).start()
                if k < chunks - 1:
                    @pl.when(even)
                    def _():
                        send_edges(f, k, True)
                else:
                    send_edges(f, k, True)

            @pl.when(section == last)
            def _():
                for r in range(rows):
                    stage[f, pl.ds(k * part * rows + r, part, stride=rows), :] = result[
                        f, r, piece(k)
                    ]
                for peer in range(k * layers // chunks, (k + 1) * layers // chunks):
                    if peer < last:
                        out_copy(f, peer).start()
                    else:
                        own_copy(f).start()

    for f in range(frames):
        for k in range(chunks):
            for side, (present, _) in enumerate(sides):
                whole = k == chunks - 1

                @pl.when(present & ((section == 0) if whole else even))
                def _():
                    edge_copy(f, k, side, False).wait_send()

                @pl.when(present & (sends_on if whole else sends_on & even))
                def _():
                    edge_copy(f, k, side, True).wait_send()

            @pl.when(section < last)
            def _():
                main_copy(f, k).wait_send()

        @pl.when(section == last)
        def _():
            for peer in range(last):
                out_copy(f, peer).wait_send()
            own_copy(f).wait()

    @pl.when(section < last)
    def _():
        for f in range(frames):
            out_copy(f, 0).wait_recv()


def local(latents, conv_weight, gain):
    frames, channels, rows, cols = latents.shape
    layers = lax.axis_size("section")
    tiles = lax.axis_size("tiles")
    share = channels // layers
    first_tap = max(0, 3 - frames)
    taps = 3 - first_tap
    chunks = 2
    depth = -(-channels // 256) * 256
    f32, bf16 = jnp.float32, jnp.bfloat16
    dma = pltpu.SemaphoreType.DMA
    macs = frames * rows * cols * channels * channels * 27
    dims = (frames, rows, channels, cols, layers, tiles, first_tap, chunks, depth)
    out = pl.pallas_call(
        functools.partial(kernel, dims),
        out_shape=jax.ShapeDtypeStruct((frames, share * rows, cols), f32),
        in_specs=[pl.BlockSpec(memory_space=pltpu.HBM)] * 3,
        out_specs=pl.BlockSpec(memory_space=pltpu.HBM),
        scratch_shapes=[
            pltpu.VMEM((frames, channels * rows, cols), f32),
            pltpu.VMEM((taps, 3, 3, channels, channels), f32),
            pltpu.VMEM((1, channels), f32),
            pltpu.VMEM((2, taps, 3 * channels, 3 * depth), bf16),
            pltpu.VMEM((frames, rows, channels, cols), f32),
            pltpu.VMEM((frames, 2, channels, cols), f32),
            pltpu.VMEM((frames, rows + 2, 2, depth, cols), bf16),
            pltpu.VMEM((frames, 3 * channels, rows * cols), f32),
            pltpu.VMEM((frames, rows, channels, cols), f32),
            pltpu.VMEM((frames, channels * rows, cols), f32),
            pltpu.VMEM((channels, cols), f32),
            dma(()),
            dma(()),
            dma((taps, 3)),
            dma((frames, chunks)),
            dma((frames, chunks)),
            dma((frames, chunks, 2, 2)),
            dma((frames, chunks, 2)),
            dma((frames, layers)),
            dma((frames,)),
            dma((frames,)),
        ],
        compiler_params=pltpu.CompilerParams(
            collective_id=0, has_side_effects=True, vmem_limit_bytes=64 * 1024 * 1024
        ),
        cost_estimate=pl.CostEstimate(
            flops=6 * macs, bytes_accessed=4 * conv_weight.size, transcendentals=latents.size
        ),
    )(latents.reshape(frames, channels * rows, cols), conv_weight, gain)
    return out.reshape(frames, share, rows, cols)


def solution(mesh):
    return jax.shard_map(
        local,
        mesh=mesh,
        in_specs=(
            P("groups", None, "tiles", None),
            P("section", None, None, None),
            P("section", None),
        ),
        out_specs=P("groups", "section", "tiles", None),
        check_vma=False,
    )
```
